32 devices in a mesh: dp: 8 (over y, x, core), pipe: 4 (over z).
Axes of the slice: x: 2, y: 2, z: 4, core: 2. Of those that a mesh axis runs over, the one named last changes fastest.
Arguments:
- hidden: bfloat16 [2048, 2048], P('dp'), may hold values from -6 to 6
- gain: float32 [2048], replicated, may hold values from 0.25 to 1.75
- w_value: bfloat16 [4, 2048, 2048], P('pipe', 'dp'), may hold values from -0.125 to 0.125
- d_value: bfloat16 [4, 2048, 2048], P('pipe', 'dp'), may hold values from -3 to 3
Outputs:
- grad_hidden: bfloat16 [2048, 2048], P('dp')
- grad_gain: float32 [2048], P('dp')
- grad_value: float32 [4, 2048, 2048], P('pipe', 'dp')
The draws below stay inside these ranges and needn't reach their ends.
All inputs are finite; a program needn't handle non-finite values.
Results may differ from the reference program's by a relative error of at most 0.0029.
Values may be sent and summed in bfloat16 or wider, within the bound.
A program may use at most 64 MiB of HBM per device.

```python
import jax
import jax.numpy as jnp
from jax import lax

D = 2048
KV = 2048
TOKENS = 2048
SECTIONS = 4
N_DP = 8


def raised(values, rng, source, target, parts, factor):
    owner, partner = [(jnp.arange(values.shape[axis_at]) // (values.shape[axis_at] // parts)).reshape([-1 if axis == axis_at else 1 for axis in range(values.ndim)]) for axis_at in (source, target)]
    chosen = jax.random.permutation(rng, parts)[partner]
    strong = (owner == chosen) | (owner == (partner + parts // 2) % parts)
    return jnp.where(strong, factor * values, values)


def steps_of(own_key, dims, shards, least, top_value):
    def one(axis_at, blocks):
        steps = jax.random.uniform(jax.random.fold_in(jax.random.fold_in(own_key, 6), axis_at), (blocks,), jnp.float32, least / len(shards), top_value / len(shards))
        return jnp.repeat(jnp.exp(steps), dims[axis_at] // blocks).reshape((-1,) + (1,) * (len(dims) - axis_at - 1))

    level = one(*shards[0])
    for cut in shards[1:]:
        level = level * one(*cut)
    return level


def noise(own_key, shape, width, bound, pieces=(), kind=jnp.bfloat16):
    array = jax.random.normal(own_key, shape, jnp.float32) * width
    if len(pieces) > 0:
        array = steps_of(own_key, shape, pieces, -0.22, 0.18) * array
    return jnp.clip(array, min=-bound, max=bound).astype(kind)


def bell_draw_with(rng, dims, scale, reach, shards, heavy, held_as=jnp.bfloat16):
    result = scale * jax.random.normal(rng, dims, jnp.float32)
    if shards:
        result = result * steps_of(rng, dims, shards, -0.22, 0.18)
    return jnp.clip(raised(result, jax.random.fold_in(rng, 3), *heavy), -reach, reach).astype(held_as)


def setup_inputs(seed: int = 0) -> dict:
    keys = jax.random.split(jax.random.key(seed), 5)
    return {
        "hidden": bell_draw_with(keys[0], (TOKENS, D), 1.0, 6.0, ((0, 8),), (0, 1, 8, 2.0)),
        "gain": jnp.clip(1.0 + 0.15 * jax.random.normal(keys[1], (D,), jnp.float32), 0.25, 1.75),
        "w_value": noise(keys[2], (SECTIONS, D, KV), D ** -0.5, 0.125, ((0, 4), (1, 8))),
        "d_value": noise(keys[3], (SECTIONS, TOKENS, KV), 0.5, 3.0, ((0, 4), (1, 8))),
    }


epsilon = 1e-06

def reference(hidden, gain, w_value, d_value):
    hidden_f = hidden.astype(jnp.float32)
    row_scale = jnp.sqrt(lax.optimization_barrier(jnp.mean(hidden_f * hidden_f, axis=-1, keepdims=True)) + epsilon)
    normed = hidden_f / row_scale
    encoded = (normed * gain).astype(jnp.bfloat16)
    grad_encoded = jnp.zeros(hidden.shape, jnp.float32)
    value_list = []
    for section in range(SECTIONS):
        grad_encoded = grad_encoded + lax.dot_general(d_value[section], w_value[section], (((1,), (1,)), ((), ())), preferred_element_type=jnp.float32)
        value_list.append(lax.dot_general(encoded, d_value[section], (((0,), (0,)), ((), ())), preferred_element_type=jnp.float32) / N_DP)
    grad_gain = lax.optimization_barrier(jnp.sum(grad_encoded * normed, axis=0)) / N_DP
    scaled = gain * grad_encoded
    grad_hidden = ((scaled - normed * lax.optimization_barrier(jnp.mean(scaled * normed, axis=-1, keepdims=True))) / row_scale).astype(jnp.bfloat16)
    return (grad_hidden, grad_gain, jnp.stack(value_list))
```

```python
import functools

import jax
import jax.numpy as jnp
from jax import lax
from jax.experimental import pallas as pl
from jax.experimental.pallas import tpu as pltpu
from jax.sharding import PartitionSpec as P

epsilon = 1e-06
MESH = pl.DeviceIdType.MESH


def norm_backward(grad_rows, normed_rows, scale_rows, gain):
    scaled = gain * grad_rows
    result = (
        scaled - normed_rows * jnp.mean(scaled * normed_rows, axis=-1, keepdims=True)
    ) / scale_rows
    return (result.astype(jnp.bfloat16), jnp.sum(grad_rows * normed_rows, axis=0))


def weight_term(encoded, operand):
    return lax.dot_general(
        encoded, operand, (((0,), (0,)), ((), ())), preferred_element_type=jnp.float32
    )


def local_general(hidden, gain, w_value, d_value):
    hidden_f = hidden.astype(jnp.float32)
    row_scale = jnp.sqrt(jnp.mean(hidden_f * hidden_f, axis=-1, keepdims=True) + epsilon)
    normed = hidden_f / row_scale
    encoded = (normed * gain).astype(jnp.bfloat16)
    cotangent = d_value[0]
    projection = w_value[0]
    average = 1.0 / lax.axis_size("dp")
    partial_value = lax.dot_general(
        cotangent,
        lax.all_gather(projection, "dp", axis=0, tiled=True),
        (((1,), (1,)), ((), ())),
        preferred_element_type=jnp.float32,
    )
    grad_rows = lax.psum_scatter(partial_value, "pipe", scatter_dimension=0, tiled=True)
    count = grad_rows.shape[0]
    first = lax.axis_index("pipe") * count
    normed_rows = lax.dynamic_slice_in_dim(normed, first, count, 0)
    scale_rows = lax.dynamic_slice_in_dim(row_scale, first, count, 0)
    hidden_part, gain_part = norm_backward(grad_rows, normed_rows, scale_rows, gain)
    grad_hidden = lax.all_gather(hidden_part, "pipe", axis=0, tiled=True)
    gain_share = lax.psum_scatter(gain_part, "dp", scatter_dimension=0, tiled=True)
    gain_share = lax.psum(gain_share, "pipe")
    grad_gain = gain_share * average
    value_grad = (
        lax.psum_scatter(weight_term(encoded, cotangent), "dp", scatter_dimension=0, tiled=True)
        * average
    )
    return (grad_hidden, grad_gain, value_grad[None])


def kernel(
    n_dp, n_pipe,
    hidden_ref, gain_ref, w_ref, d_ref,
    hidden_out, gain_out, value_out,
    d_all, part, recv1, sum1, recv2, final, rows, enc, enc_cols, hid_all,
    gain_part, gain_recv, gain_sum, gain_z,
    own_sem, x_send, x_recv, y_send, y_recv, s_send, s_recv,
    enc_send, enc_recv, one_send, one_recv, two_send, two_recv,
    row_send, row_recv, hid_send, hid_recv, gp_send, gp_recv, gz_send, gz_recv,
):
    me = lax.axis_index("dp")
    z = lax.axis_index("pipe")
    core = me % 2
    side_x = (me // 2) % 2
    side_y = me // 4
    step_s, step_x, step_y = 1 - 2 * core, 2 - 4 * side_x, 4 - 8 * side_y
    at_s, at_x, at_y, at_d = me + step_s, me + step_x, me + step_y, me + step_x + step_y
    parity, half_own = z % 2, z // 2
    z_one = z + 1 - 2 * parity
    z_two = z + 2 - 4 * half_own
    chunk, width = rows.shape[1], rows.shape[2]
    model = gain_ref.shape[-1]

    barrier = pltpu.get_barrier_semaphore()
    for k in range(1, n_dp):
        pl.semaphore_signal(barrier, inc=1, device_id=((me + k) % n_dp, z), device_id_type=MESH)
    for other in (z_one, z_two):
        pl.semaphore_signal(barrier, inc=1, device_id=(me, other), device_id_type=MESH)
    pl.semaphore_wait(barrier, n_dp - 1 + 2)

    sent = []

    def send(src, dst, send_sem, recv_sem, target):
        copy = pltpu.make_async_remote_copy(
            src_ref=src, dst_ref=dst, send_sem=send_sem, recv_sem=recv_sem,
            device_id=target, device_id_type=MESH,
        )
        copy.start()
        sent.append(copy)

    def arrived(dst, recv_sem):
        pltpu.make_async_remote_copy(
            src_ref=dst, dst_ref=dst, send_sem=recv_sem, recv_sem=recv_sem,
            device_id=(me, z_one), device_id_type=MESH,
        ).wait_recv()

    send(d_ref.at[0], d_all.at[me, 0], x_send.at[0], x_recv.at[0], (at_x, z))
    send(d_ref.at[1], d_all.at[me, 1], y_send.at[1], y_recv.at[1], (at_y, z))
    send(d_ref.at[0], d_all.at[me, 0], s_send.at[0, 0], s_recv.at[0, 0], (at_s, z))
    send(d_ref.at[1], d_all.at[me, 1], s_send.at[0, 1], s_recv.at[0, 1], (at_s, z))
    send(d_ref.at[1], d_all.at[me, 1], x_send.at[1], x_recv.at[1], (at_x, z))
    send(d_ref.at[0], d_all.at[me, 0], y_send.at[0], y_recv.at[0], (at_y, z))
    own = pltpu.make_async_copy(d_ref, d_all.at[me], own_sem)
    own.start()

    def process(block, origin, half):
        product = lax.dot_general(
            block, w_ref[...], (((1,), (1,)), ((), ())), preferred_element_type=jnp.float32
        )
        part[origin, half] = product.reshape(2, chunk, width)
        send(
            part.at[origin, half, 1 - parity], recv1.at[origin, half],
            one_send.at[origin, half], one_recv.at[origin, half], (me, z_one),
        )

    def arrive_process(origin, half):
        process(d_all[origin, half], origin, half)

    def share(kind, origin, half):
        send(
            d_all.at[origin, half], d_all.at[origin, half],
            s_send.at[kind, half], s_recv.at[kind, half], (at_s, z),
        )

    def first_sum(origin):
        for half, goes in ((1 - half_own, True), (half_own, False)):
            arrived(recv1.at[origin, half], one_recv.at[origin, half])
            total = part[origin, half, parity] + recv1[origin, half]
            if goes:
                sum1[origin] = total
                send(
                    sum1.at[origin], recv2.at[origin],
                    two_send.at[origin], two_recv.at[origin], (me, z_two),
                )
            else:
                part[origin, half, parity] = total

    def second_sum(origin, mine):
        arrived(recv2.at[origin], two_recv.at[origin])
        total = part[origin, half_own, parity] + recv2[origin]
        if mine:
            rows[me] = total
        else:
            final[origin] = total
            send(
                final.at[origin], rows.at[me],
                row_send.at[origin], row_recv.at[me], (origin, z),
            )

    process(d_ref[0], me, 0)
    process(d_ref[1], me, 1)
    for half in range(2):
        arrived(d_all.at[at_s, half], s_recv.at[0, half])
        arrive_process(at_s, half)

    def scale_of(block):
        return jnp.sqrt(jnp.mean(block * block, axis=-1, keepdims=True) + epsilon)

    for q in range(n_pipe):
        block = hidden_ref[q].astype(jnp.float32)
        value = (block * (1.0 / scale_of(block)) * gain_ref[...]).astype(jnp.bfloat16)
        for j in range(n_dp):
            enc[j, q] = value[:, j * width:(j + 1) * width]
    enc_cols[me] = enc[me]

    arrived(d_all.at[at_x, 0], x_recv.at[0])
    send(d_all.at[at_x, 0], d_all.at[at_x, 0], y_send.at[2], y_recv.at[2], (at_y, z))
    share(1, at_x, 0)
    arrived(d_all.at[at_y, 1], y_recv.at[1])
    send(d_all.at[at_y, 1], d_all.at[at_y, 1], x_send.at[2], x_recv.at[2], (at_x, z))
    share(2, at_y, 1)
    arrive_process(at_x, 0)
    arrive_process(at_y, 1)
    arrived(d_all.at[at_x + step_s, 0], s_recv.at[1, 0])
    arrive_process(at_x + step_s, 0)
    arrived(d_all.at[at_y + step_s, 1], s_recv.at[2, 1])
    arrive_process(at_y + step_s, 1)
    first_sum(me)
    first_sum(at_s)

    arrived(d_all.at[at_x, 1], x_recv.at[1])
    share(1, at_x, 1)
    arrived(d_all.at[at_y, 0], y_recv.at[0])
    share(2, at_y, 0)
    for k in range(1, n_dp):
        to = (me + k) % n_dp
        send(enc.at[to], enc_cols.at[me], enc_send.at[to], enc_recv.at[me], (to, z))
    arrive_process(at_x, 1)
    arrive_process(at_y, 0)
    arrived(d_all.at[at_x + step_s, 1], s_recv.at[1, 1])
    arrive_process(at_x + step_s, 1)
    arrived(d_all.at[at_y + step_s, 0], s_recv.at[2, 0])
    arrive_process(at_y + step_s, 0)
    second_sum(me, True)
    second_sum(at_s, False)
    for origin in (at_x, at_y, at_x + step_s, at_y + step_s):
        first_sum(origin)

    arrived(d_all.at[at_d, 0], y_recv.at[2])
    share(3, at_d, 0)
    arrived(d_all.at[at_d, 1], x_recv.at[2])
    share(3, at_d, 1)
    arrive_process(at_d, 0)
    arrive_process(at_d, 1)
    for half in range(2):
        arrived(d_all.at[at_d + step_s, half], s_recv.at[3, half])
        arrive_process(at_d + step_s, half)
    for origin in (at_x, at_y, at_x + step_s, at_y + step_s):
        second_sum(origin, False)
    first_sum(at_d)
    first_sum(at_d + step_s)
    second_sum(at_d, False)
    second_sum(at_d + step_s, False)

    block = hidden_ref[z].astype(jnp.float32)
    inverse = 1.0 / scale_of(block)
    for k in range(1, n_dp):
        source = (me + k) % n_dp
        arrived(rows.at[source], row_recv.at[source])
    dots = jnp.zeros((chunk, 1), jnp.float32)
    for j in range(n_dp):
        columns = slice(j * width, (j + 1) * width)
        normed = hidden_ref[z, :, columns].astype(jnp.float32) * inverse
        product = rows[j] * normed
        dots += jnp.sum(product * gain_ref[:, columns], axis=-1, keepdims=True)
        gain_part[j] = jnp.sum(product.reshape(chunk // 8, 8, width), axis=0)
    dots = dots * (1.0 / model)
    for j in range(n_dp):
        columns = slice(j * width, (j + 1) * width)
        normed = hidden_ref[z, :, columns].astype(jnp.float32) * inverse
        scaled = rows[j] * gain_ref[:, columns]
        hid_all[z, :, columns] = ((scaled - normed * dots) * inverse).astype(jnp.bfloat16)
    send(hid_all.at[z], hid_all.at[z], hid_send.at[0], hid_recv.at[0], (me, z_two))
    send(hid_all.at[z], hid_all.at[z], hid_send.at[1], hid_recv.at[1], (me, z_one))
    gain_recv[me] = gain_part[me]
    for k in range(1, n_dp):
        to = (me + k) % n_dp
        send(gain_part.at[to], gain_recv.at[me], gp_send.at[to], gp_recv.at[me], (to, z))

    for k in range(1, n_dp):
        source = (me + k) % n_dp
        arrived(enc_cols.at[source], enc_recv.at[source])
    own.wait()
    count = n_dp * 2 * d_all.shape[2]
    tile = 2 * width

    def value_tiles(first, last):
        def body(t, carry):
            columns = pl.ds(pl.multiple_of(t * tile, tile), tile)
            value_out[:, columns] = lax.dot_general(
                enc_cols[...].reshape(count, width),
                d_all[:, :, :, columns].reshape(count, tile),
                (((0,), (0,)), ((), ())),
                preferred_element_type=jnp.float32,
            )
            return carry

        lax.fori_loop(first, last, body, 0)

    tiles = d_all.shape[-1] // tile
    for k in range(1, n_dp):
        source = (me + k) % n_dp
        arrived(gain_recv.at[source], gp_recv.at[source])
    gain_sum[0] = jnp.sum(gain_recv[...], axis=0)
    send(gain_sum.at[0], gain_z.at[0], gz_send.at[0], gz_recv.at[0], (me, z_one))
    value_tiles(0, tiles // 2)
    arrived(gain_z.at[0], gz_recv.at[0])
    gain_sum[1] = gain_sum[0] + gain_z[0]
    send(gain_sum.at[1], gain_z.at[1], gz_send.at[1], gz_recv.at[1], (me, z_two))
    arrived(hid_all.at[z_two], hid_recv.at[0])
    send(hid_all.at[z_two], hid_all.at[z_two], hid_send.at[2], hid_recv.at[2], (me, z_one))
    value_tiles(tiles // 2, tiles)
    arrived(gain_z.at[1], gz_recv.at[1])
    gain_out[...] = jnp.sum(gain_sum[1] + gain_z[1], axis=0, keepdims=True) * (1.0 / n_dp)
    arrived(hid_all.at[z_one], hid_recv.at[1])
    arrived(hid_all.at[z_one + z_two - z], hid_recv.at[2])
    hidden_out[...] = hid_all[...]
    for copy in sent:
        copy.wait_send()


def local_cube(n_dp, n_pipe, hidden, gain, w_value, d_value):
    tokens, model = hidden.shape
    kv = d_value.shape[-1]
    width = w_value.shape[1]
    chunk = tokens // n_pipe
    f32, bf16 = jnp.float32, jnp.bfloat16
    dma = pltpu.SemaphoreType.DMA
    vmem = pl.BlockSpec(memory_space=pltpu.VMEM)
    flops = 4 * n_dp * tokens * width * kv
    hidden_grad, gain_grad, value_grad = pl.pallas_call(
        functools.partial(kernel, n_dp, n_pipe),
        out_shape=(
            jax.ShapeDtypeStruct((n_pipe, chunk, model), bf16),
            jax.ShapeDtypeStruct((1, width), f32),
            jax.ShapeDtypeStruct((width, kv), f32),
        ),
        in_specs=[vmem] * 4,
        out_specs=(vmem, vmem, vmem),
        scratch_shapes=[
            pltpu.VMEM((n_dp, 2, 2 * chunk, kv), bf16),
            pltpu.VMEM((n_dp, 2, 2, chunk, width), f32),
            pltpu.VMEM((n_dp, 2, chunk, width), f32),
            pltpu.VMEM((n_dp, chunk, width), f32),
            pltpu.VMEM((n_dp, chunk, width), f32),
            pltpu.VMEM((n_dp, chunk, width), f32),
            pltpu.VMEM((n_dp, chunk, width), f32),
            pltpu.VMEM((n_dp, n_pipe, chunk, width), bf16),
            pltpu.VMEM((n_dp, n_pipe, chunk, width), bf16),
            pltpu.VMEM((n_pipe, chunk, model), bf16),
            pltpu.VMEM((n_dp, 8, width), f32),
            pltpu.VMEM((n_dp, 8, width), f32),
            pltpu.VMEM((2, 8, width), f32),
            pltpu.VMEM((2, 8, width), f32),
            dma(()),
            dma((3,)), dma((3,)), dma((3,)), dma((3,)),
            dma((4, 2)), dma((4, 2)),
            dma((n_dp,)), dma((n_dp,)),
            dma((n_dp, 2)), dma((n_dp, 2)),
            dma((n_dp,)), dma((n_dp,)),
            dma((n_dp,)), dma((n_dp,)),
            dma((3,)), dma((3,)),
            dma((n_dp,)), dma((n_dp,)),
            dma((2,)), dma((2,)),
        ],
        compiler_params=pltpu.CompilerParams(
            collective_id=0, has_side_effects=True, vmem_limit_bytes=50 * 2**20
        ),
        cost_estimate=pl.CostEstimate(flops=flops, bytes_accessed=8 * 2**20, transcendentals=0),
    )(
        hidden.reshape(n_pipe, chunk, model),
        gain.reshape(1, model),
        w_value[0],
        d_value[0].reshape(2, 2 * chunk, kv),
    )
    return (
        hidden_grad.reshape(tokens, model),
        gain_grad.reshape(width),
        (value_grad * (1.0 / n_dp))[None],
    )


def solution(mesh):
    n_dp, n_pipe = mesh.shape["dp"], mesh.shape["pipe"]

    def local(hidden, gain, w_value, d_value):
        tokens, model = hidden.shape
        width = w_value.shape[1]
        cube = n_dp == 2 * 2 * 2 and n_pipe == 2 * 2
        fits = tokens % (16 * n_pipe) == 0 and width % 128 == 0 and model == n_dp * width
        fits = fits and d_value.shape[-1] % (4 * width) == 0 and n_dp * tokens <= model
        if cube and fits:
            return local_cube(n_dp, n_pipe, hidden, gain, w_value, d_value)
        return local_general(hidden, gain, w_value, d_value)

    return jax.shard_map(
        local,
        mesh=mesh,
        in_specs=(P("dp", None), P(), P("pipe", "dp", None), P("pipe", "dp", None)),
        out_specs=(P("dp", None), P("dp"), P("pipe", "dp", None)),
        check_vma=False,
    )
```

```python
import functools

import jax
import jax.numpy as jnp
from jax import lax
from jax.experimental import pallas as pl
from jax.experimental.pallas import tpu as pltpu
from jax.sharding import PartitionSpec as P

epsilon = 1e-06
MESH = pl.DeviceIdType.MESH


def norm_backward(grad_rows, normed_rows, scale_rows, gain):
    scaled = gain * grad_rows
    result = (
        scaled - normed_rows * jnp.mean(scaled * normed_rows, axis=-1, keepdims=True)
    ) / scale_rows
    return (result.astype(jnp.bfloat16), jnp.sum(grad_rows * normed_rows, axis=0))


def weight_term(encoded, operand):
    return lax.dot_general(
        encoded, operand, (((0,), (0,)), ((), ())), preferred_element_type=jnp.float32
    )


def local_general(hidden, gain, w_value, d_value):
    hidden_f = hidden.astype(jnp.float32)
    row_scale = jnp.sqrt(jnp.mean(hidden_f * hidden_f, axis=-1, keepdims=True) + epsilon)
    normed = hidden_f / row_scale
    encoded = (normed * gain).astype(jnp.bfloat16)
    cotangent = d_value[0]
    projection = w_value[0]
    average = 1.0 / lax.axis_size("dp")
    partial_value = lax.dot_general(
        cotangent,
        lax.all_gather(projection, "dp", axis=0, tiled=True),
        (((1,), (1,)), ((), ())),
        preferred_element_type=jnp.float32,
    )
    grad_rows = lax.psum_scatter(partial_value, "pipe", scatter_dimension=0, tiled=True)
    count = grad_rows.shape[0]
    first = lax.axis_index("pipe") * count
    normed_rows = lax.dynamic_slice_in_dim(normed, first, count, 0)
    scale_rows = lax.dynamic_slice_in_dim(row_scale, first, count, 0)
    hidden_part, gain_part = norm_backward(grad_rows, normed_rows, scale_rows, gain)
    grad_hidden = lax.all_gather(hidden_part, "pipe", axis=0, tiled=True)
    gain_share = lax.psum_scatter(gain_part, "dp", scatter_dimension=0, tiled=True)
    gain_share = lax.psum(gain_share, "pipe")
    grad_gain = gain_share * average
    value_grad = (
        lax.psum_scatter(weight_term(encoded, cotangent), "dp", scatter_dimension=0, tiled=True)
        * average
    )
    return (grad_hidden, grad_gain, value_grad[None])


def kernel(
    n_dp, n_pipe,
    hidden_hbm, gain_hbm, w_hbm, d_hbm,
    hidden_out, gain_out, value_out,
    hidden_ref, gain_ref, w_ref, value_ref,
    d_all, part, out1, recv1, sum1, recv2, final, rows, enc, enc_cols,
    gain_part, gain_recv, gain_sum, gain_z,
    own_sem, x_send, x_recv, y_send, y_recv, s_send, s_recv,
    enc_send, enc_recv, one_send, one_recv, two_send, two_recv,
    row_send, row_recv, hid_send, hid_recv, gp_send, gp_recv, gz_send, gz_recv,
):
    me = lax.axis_index("dp")
    z = lax.axis_index("pipe")
    core = me % 2
    side_x = (me // 2) % 2
    side_y = me // 4
    step_s, step_x, step_y = 1 - 2 * core, 2 - 4 * side_x, 4 - 8 * side_y
    at_s, at_x, at_y, at_d = me + step_s, me + step_x, me + step_y, me + step_x + step_y
    parity, half_own = z % 2, z // 2
    z_one = z + 1 - 2 * parity
    z_two = z + 2 - 4 * half_own
    chunk, width = rows.shape[2], rows.shape[3]
    model = gain_ref.shape[-1]

    own = pltpu.make_async_copy(d_hbm, d_all.at[me], own_sem.at[0])
    load_w = pltpu.make_async_copy(w_hbm, w_ref, own_sem.at[1])
    load_h = pltpu.make_async_copy(hidden_hbm, hidden_ref, own_sem.at[2])
    load_g = pltpu.make_async_copy(gain_hbm, gain_ref, own_sem.at[3])
    for copy in (own, load_w, load_h, load_g):
        copy.start()

    barrier = pltpu.get_barrier_semaphore()
    for k in range(1, n_dp):
        pl.semaphore_signal(barrier, inc=1, device_id=((me + k) % n_dp, z), device_id_type=MESH)
    for other in (z_one, z_two):
        pl.semaphore_signal(barrier, inc=1, device_id=(me, other), device_id_type=MESH)
    pl.semaphore_wait(barrier, n_dp - 1 + 2)

    sent = []

    def send(src, dst, send_sem, recv_sem, target):
        copy = pltpu.make_async_remote_copy(
            src_ref=src, dst_ref=dst, send_sem=send_sem, recv_sem=recv_sem,
            device_id=target, device_id_type=MESH,
        )
        copy.start()
        sent.append(copy)

    def arrived(dst, recv_sem):
        pltpu.make_async_remote_copy(
            src_ref=dst, dst_ref=dst, send_sem=recv_sem, recv_sem=recv_sem,
            device_id=(me, z_one), device_id_type=MESH,
        ).wait_recv()

    def own_x(sub, half):
        send(d_hbm.at[sub, half], d_all.at[me, sub, half],
             x_send.at[sub, half], x_recv.at[sub, half], (at_x, z))

    def own_y(sub, half):
        send(d_hbm.at[sub, half], d_all.at[me, sub, half],
             y_send.at[sub, half], y_recv.at[sub, half], (at_y, z))

    def own_s(sub, half):
        send(d_hbm.at[sub, half], d_all.at[me, sub, half],
             s_send.at[sub, 0, half], s_recv.at[sub, 0, half], (at_s, z))

    def share(sub, kind, origin, half):
        send(d_all.at[origin, sub, half], d_all.at[origin, sub, half],
             s_send.at[sub, kind, half], s_recv.at[sub, kind, half], (at_s, z))

    def product(sub, *blocks):
        joined = jnp.concatenate([d_all[origin, sub, half] for origin, half in blocks], axis=0)
        result = lax.dot_general(
            joined, w_ref[...], (((1,), (1,)), ((), ())), preferred_element_type=jnp.float32
        )
        count = 2 * chunk
        for k, (origin, half) in enumerate(blocks):
            part[origin, sub, half] = result[k * count:(k + 1) * count].reshape(2, chunk, width)
            out1[origin, sub, half] = part[origin, sub, half, 1 - parity].astype(jnp.bfloat16)
            send(
                out1.at[origin, sub, half], recv1.at[origin, sub, half],
                one_send.at[origin, sub, half], one_recv.at[origin, sub, half], (me, z_one),
            )

    def first_sum(sub, *origins):
        for origin in origins:
            goes, stays = 1 - half_own, half_own
            arrived(recv1.at[origin, sub, goes], one_recv.at[origin, sub, goes])
            sum1[origin, sub] = (
                part[origin, sub, goes, parity] + recv1[origin, sub, goes].astype(jnp.float32)
            )
            send(
                sum1.at[origin, sub], recv2.at[origin, sub],
                two_send.at[origin, sub], two_recv.at[origin, sub], (me, z_two),
            )
            arrived(recv1.at[origin, sub, stays], one_recv.at[origin, sub, stays])

    def second_sum(sub, *origins):
        for origin in origins:
            arrived(recv2.at[origin, sub], two_recv.at[origin, sub])
            kept = recv1[origin, sub, half_own].astype(jnp.float32)
            total = part[origin, sub, half_own, parity] + kept + recv2[origin, sub]
            if origin is me:
                rows[me, sub] = total
            else:
                final[origin, sub] = total
                send(
                    final.at[origin, sub], rows.at[me, sub],
                    row_send.at[origin, sub], row_recv.at[me, sub], (origin, z),
                )

    def scale_of(block):
        return jnp.sqrt(jnp.mean(block * block, axis=-1, keepdims=True) + epsilon)

    def gather_first(sub):
        arrived(d_all.at[at_x, sub, 0], x_recv.at[sub, 0])
        send(d_all.at[at_x, sub, 0], d_all.at[at_x, sub, 0],
             y_send.at[sub, 2], y_recv.at[sub, 2], (at_y, z))
        share(sub, 1, at_x, 0)
        arrived(d_all.at[at_y, sub, 1], y_recv.at[sub, 1])
        send(d_all.at[at_y, sub, 1], d_all.at[at_y, sub, 1],
             x_send.at[sub, 2], x_recv.at[sub, 2], (at_x, z))
        share(sub, 2, at_y, 1)

    def gather_second(sub):
        arrived(d_all.at[at_x, sub, 1], x_recv.at[sub, 1])
        share(sub, 1, at_x, 1)
        arrived(d_all.at[at_y, sub, 0], y_recv.at[sub, 0])
        share(sub, 2, at_y, 0)

    def gather_third(sub):
        arrived(d_all.at[at_d, sub, 0], y_recv.at[sub, 2])
        share(sub, 3, at_d, 0)
        arrived(d_all.at[at_d, sub, 1], x_recv.at[sub, 2])
        share(sub, 3, at_d, 1)

    def products(sub, *kinds):
        product(sub, *[((at_x, at_y, at_d)[kind - 1], half) for kind, half in kinds])
        siblings = [((at_x, at_y, at_d)[kind - 1] + step_s, half) for kind, half in kinds]
        for (kind, half), (origin, _) in zip(kinds, siblings):
            arrived(d_all.at[origin, sub, half], s_recv.at[sub, kind, half])
        product(sub, *siblings)

    sides = (at_x, at_y, at_x + step_s, at_y + step_s)
    corners = (at_d, at_d + step_s)
    pair = (me, at_s)

    def send_encoded(*targets):
        for to in targets:
            send(enc.at[to], enc_cols.at[me], enc_send.at[to], enc_recv.at[me], (to, z))

    def norm_part(sub):
        block = hidden_ref[sub, z].astype(jnp.float32)
        inverse = 1.0 / scale_of(block)
        for k in range(1, n_dp):
            source = (me + k) % n_dp
            arrived(rows.at[source, sub], row_recv.at[source, sub])
        dots = jnp.zeros((chunk, 1), jnp.float32)
        for j in range(n_dp):
            columns = slice(j * width, (j + 1) * width)
            normed = hidden_ref[sub, z, :, columns].astype(jnp.float32) * inverse
            term = rows[j, sub] * normed
            dots += jnp.sum(term * gain_ref[:, columns], axis=-1, keepdims=True)
            folded = jnp.sum(term.reshape(chunk // 8, 8, width), axis=0)
            gain_part[j] = folded if sub == 0 else gain_part[j] + folded
        dots = dots * (1.0 / model)
        for j in range(n_dp):
            columns = slice(j * width, (j + 1) * width)
            normed = hidden_ref[sub, z, :, columns].astype(jnp.float32) * inverse
            scaled = rows[j, sub] * gain_ref[:, columns]
            hidden_out[sub, z, :, columns] = ((scaled - normed * dots) * inverse).astype(
                jnp.bfloat16
            )
        mine = hidden_out.at[sub, z]
        send(mine, mine, hid_send.at[sub, 0], hid_recv.at[sub, 0], (me, z_two))
        send(mine, mine, hid_send.at[sub, 1], hid_recv.at[sub, 1], (me, z_one))

    def norm_pass_on(sub):
        theirs = hidden_out.at[sub, z_two]
        arrived(theirs, hid_recv.at[sub, 0])
        send(theirs, theirs, hid_send.at[sub, 2], hid_recv.at[sub, 2], (me, z_one))

    def norm_end(sub):
        arrived(hidden_out.at[sub, z_one], hid_recv.at[sub, 1])
        arrived(hidden_out.at[sub, z_one + z_two - z], hid_recv.at[sub, 2])

    own_x(0, 0)
    own_y(0, 1)
    own_s(0, 0)
    own_s(0, 1)
    own_x(0, 1)
    own_y(0, 0)
    own_s(1, 0)
    own_s(1, 1)
    load_w.wait()
    own.wait()
    for sub in range(2):
        product(sub, (me, 0), (me, 1))
        for half in range(2):
            arrived(d_all.at[at_s, sub, half], s_recv.at[sub, 0, half])
        product(sub, (at_s, 0), (at_s, 1))

    load_h.wait()
    load_g.wait()
    for sub in range(2):
        for q in range(n_pipe):
            block = hidden_ref[sub, q].astype(jnp.float32)
            value = (block * (1.0 / scale_of(block)) * gain_ref[...]).astype(jnp.bfloat16)
            for j in range(n_dp):
                enc[j, sub, q] = value[:, j * width:(j + 1) * width]
    enc_cols[me] = enc[me]
    send_encoded(at_s)

    gather_first(0)
    own_x(1, 0)
    own_y(1, 1)
    products(0, (1, 0), (2, 1))
    gather_second(0)
    own_x(1, 1)
    own_y(1, 0)
    products(0, (1, 1), (2, 0))
    first_sum(0, *pair)
    gather_third(0)
    products(0, (3, 0), (3, 1))
    gather_first(1)
    products(1, (1, 0), (2, 1))
    first_sum(0, *sides)
    second_sum(0, *pair)
    gather_second(1)
    products(1, (1, 1), (2, 0))
    first_sum(0, *corners)
    first_sum(1, *pair)
    second_sum(0, *sides)
    second_sum(0, *corners)
    first_sum(1, *sides)
    second_sum(1, *pair)
    gather_third(1)
    products(1, (3, 0), (3, 1))
    send_encoded(*sides)
    norm_part(0)
    first_sum(1, *corners)
    second_sum(1, *sides)
    norm_pass_on(0)
    second_sum(1, *corners)
    send_encoded(*corners)
    norm_part(1)
    gain_recv[me] = gain_part[me]
    for k in range(1, n_dp):
        to = (me + k) % n_dp
        send(gain_part.at[to], gain_recv.at[me], gp_send.at[to], gp_recv.at[me], (to, z))

    count = 2 * enc_cols.shape[1] * enc_cols.shape[2] * enc_cols.shape[3]
    tile = 2 * width
    tiles = d_all.shape[-1] // tile
    stores = []

    def value_term(step, near, far):
        for source in (near, far):
            if source is not me:
                arrived(enc_cols.at[source], enc_recv.at[source])
        encoded = jnp.concatenate(
            [enc_cols[source].reshape(count // 2, width) for source in (near, far)], axis=0
        )
        for t in range(tiles):
            columns = slice(t * tile, (t + 1) * tile)
            operand = jnp.concatenate(
                [d_all[source, :, :, :, columns].reshape(count // 2, tile) for source in (near, far)],
                axis=0,
            )
            term = lax.dot_general(
                encoded, operand, (((0,), (0,)), ((), ())), preferred_element_type=jnp.float32
            )
            if step > 0:
                term = value_ref[:, columns] + term
            if step < 3:
                value_ref[:, columns] = term
            else:
                value_ref[:, columns] = term * (1.0 / n_dp)
                store = pltpu.make_async_copy(
                    value_ref.at[:, columns], value_out.at[:, columns], own_sem.at[4 + t]
                )
                store.start()
                stores.append(store)

    value_term(0, me, at_s)
    for k in range(1, n_dp):
        source = (me + k) % n_dp
        arrived(gain_recv.at[source], gp_recv.at[source])
    gain_sum[0] = jnp.sum(gain_recv[...], axis=0)
    send(gain_sum.at[0], gain_z.at[0], gz_send.at[0], gz_recv.at[0], (me, z_one))
    value_term(1, at_x, at_x + step_s)
    arrived(gain_z.at[0], gz_recv.at[0])
    gain_sum[1] = gain_sum[0] + gain_z[0]
    send(gain_sum.at[1], gain_z.at[1], gz_send.at[1], gz_recv.at[1], (me, z_two))
    value_term(2, at_y, at_y + step_s)
    norm_pass_on(1)
    value_term(3, at_d, at_d + step_s)
    arrived(gain_z.at[1], gz_recv.at[1])
    gain_out[...] = jnp.sum(gain_sum[1] + gain_z[1], axis=0, keepdims=True) * (1.0 / n_dp)
    norm_end(0)
    norm_end(1)
    for copy in sent:
        copy.wait_send()
    for store in stores:
        store.wait()


def local_cube(n_dp, n_pipe, hidden, gain, w_value, d_value):
    tokens, model = hidden.shape
    kv = d_value.shape[-1]
    width = w_value.shape[1]
    chunk = tokens // (2 * n_pipe)
    f32, bf16 = jnp.float32, jnp.bfloat16
    dma = pltpu.SemaphoreType.DMA
    vmem = pl.BlockSpec(memory_space=pltpu.VMEM)
    hbm = pl.BlockSpec(memory_space=pltpu.HBM)
    flops = 4 * n_dp * tokens * width * kv
    hidden_grad, gain_grad, value_grad = pl.pallas_call(
        functools.partial(kernel, n_dp, n_pipe),
        out_shape=(
            jax.ShapeDtypeStruct((2, n_pipe, chunk, model), bf16),
            jax.ShapeDtypeStruct((1, width), f32),
            jax.ShapeDtypeStruct((width, kv), f32),
        ),
        in_specs=[hbm] * 4,
        out_specs=(vmem, vmem, hbm),
        scratch_shapes=[
            pltpu.VMEM((2, n_pipe, chunk, model), bf16),
            pltpu.VMEM((1, model), f32),
            pltpu.VMEM((width, kv), bf16),
            pltpu.VMEM((width, kv), f32),
            pltpu.VMEM((n_dp, 2, 2, 2 * chunk, kv), bf16),
            pltpu.VMEM((n_dp, 2, 2, 2, chunk, width), f32),
            pltpu.VMEM((n_dp, 2, 2, chunk, width), bf16),
            pltpu.VMEM((n_dp, 2, 2, chunk, width), bf16),
            pltpu.VMEM((n_dp, 2, chunk, width), f32),
            pltpu.VMEM((n_dp, 2, chunk, width), f32),
            pltpu.VMEM((n_dp, 2, chunk, width), f32),
            pltpu.VMEM((n_dp, 2, chunk, width), f32),
            pltpu.VMEM((n_dp, 2, n_pipe, chunk, width), bf16),
            pltpu.VMEM((n_dp, 2, n_pipe, chunk, width), bf16),
            pltpu.VMEM((n_dp, 8, width), f32),
            pltpu.VMEM((n_dp, 8, width), f32),
            pltpu.VMEM((2, 8, width), f32),
            pltpu.VMEM((2, 8, width), f32),
            dma((4 + kv // (2 * width),)),
            dma((2, 3)), dma((2, 3)), dma((2, 3)), dma((2, 3)),
            dma((2, 4, 2)), dma((2, 4, 2)),
            dma((n_dp,)), dma((n_dp,)),
            dma((n_dp, 2, 2)), dma((n_dp, 2, 2)),
            dma((n_dp, 2)), dma((n_dp, 2)),
            dma((n_dp, 2)), dma((n_dp, 2)),
            dma((2, 3)), dma((2, 3)),
            dma((n_dp,)), dma((n_dp,)),
            dma((2,)), dma((2,)),
        ],
        compiler_params=pltpu.CompilerParams(
            collective_id=0, has_side_effects=True, vmem_limit_bytes=60 * 2**20
        ),
        cost_estimate=pl.CostEstimate(flops=flops, bytes_accessed=8 * 2**20, transcendentals=0),
    )(
        hidden.reshape(2, n_pipe, chunk, model),
        gain.reshape(1, model),
        w_value[0],
        d_value[0].reshape(2, 2, 2 * chunk, kv),
    )
    return (hidden_grad.reshape(tokens, model), gain_grad.reshape(width), value_grad[None])


def solution(mesh):
    n_dp, n_pipe = mesh.shape["dp"], mesh.shape["pipe"]

    def local(hidden, gain, w_value, d_value):
        tokens, model = hidden.shape
        width = w_value.shape[1]
        cube = n_dp == 2 * 2 * 2 and n_pipe == 2 * 2
        fits = tokens % (32 * n_pipe) == 0 and width % 128 == 0 and model == n_dp * width
        fits = fits and d_value.shape[-1] % (4 * width) == 0 and n_dp * tokens <= model
        if cube and fits:
            return local_cube(n_dp, n_pipe, hidden, gain, w_value, d_value)
        return local_general(hidden, gain, w_value, d_value)

    return jax.shard_map(
        local,
        mesh=mesh,
        in_specs=(P("dp", None), P(), P("pipe", "dp", None), P("pipe", "dp", None)),
        out_specs=(P("dp", None), P("dp"), P("pipe", "dp", None)),
        check_vma=False,
    )
```
